32 devices in a mesh: dom: 8 (over y, x, core), feat: 4 (over z).
Axes of the slice: x: 2, y: 2, z: 4, core: 2. Of those that a mesh axis runs over, the one named last changes fastest.
Arguments:
- features: bfloat16 [128, 65536], P('feat', 'dom'), may hold values from -6 to 6
- w1_self: bfloat16 [128, 256], replicated, may hold values from -0.5 to 0.5
- w1_neigh: bfloat16 [128, 256], replicated, may hold values from -0.5 to 0.5
- b1: float32 [256], replicated, may hold values from -3 to 3
- w2_self: bfloat16 [256, 256], replicated, may hold values from -0.375 to 0.375
- w2_neigh: bfloat16 [256, 256], replicated, may hold values from -0.046875 to 0.046875
- b2: float32 [256], replicated, may hold values from -3 to 3
- col_tiles: int32 [512, 32], P(('dom', 'feat')), may hold values from -1 to 511, as said below
- edge_weights: bfloat16 [512, 32, 128, 128], P(('dom', 'feat')), may hold values from 0 to 4, as said below
- cotangent: bfloat16 [65536, 256], P(('dom', 'feat')), may hold values from -0.0625 to 0.0625
Outputs:
- embedding: bfloat16 [65536, 256], P(('dom', 'feat'))
- grad_w2_self: float32 [256, 256], replicated
- grad_w2_neigh: float32 [256, 256], replicated
- grad_b2: float32 [256], replicated
The draws below stay inside these ranges and needn't reach their ends.
Inputs may be any that keep to these rules, and one draw needn't show every extreme that they name: Partition p holds row tiles p * 64 to (p + 1) * 64 - 1. In each row of col_tiles the live entries come first and the rest are -1; at least one entry of a row is live, and some row has all 32 live. A live entry names a tile of the row tile's own partition or of one of the two partitions beside it, the first and last partitions being beside each other. `edge_weights`: zero where two nodes share no edge.
All inputs are finite; a program needn't handle non-finite values.
Results may differ from the reference program's by a relative error of at most 0.005.
Values may be sent and summed in bfloat16 or wider, within the bound.
A program may use at most 128 MiB of HBM per device.

```python
import math
import jax
import jax.numpy as jnp
from jax import lax

F = 128
H = 256
K = 32
TOKENS = 65536
ROW_TILES = 512
PANEL_TILES = 64


def draw_col_tiles(key, part):
    key = jax.random.fold_in(key, 11)
    key_heavy, key_light, key_full, key_chosen, key_offset = jax.random.split(key, 5)
    partitions = ROW_TILES // PANEL_TILES
    heavy_part = jax.random.randint(key_heavy, (partitions,), 0, 4) == 0
    row_partition = jnp.arange(ROW_TILES, dtype=jnp.int32) // PANEL_TILES
    half_slots = K // 2
    light_count = jax.random.randint(key_light, (ROW_TILES,), 1, half_slots + 1)
    heavy_count = jax.random.randint(key_full, (ROW_TILES,), half_slots, K + 1)
    counts = jnp.where(heavy_part[row_partition], heavy_count, light_count)
    chosen = jax.random.randint(key_chosen, (), 0, ROW_TILES)
    counts = jnp.where(jnp.arange(ROW_TILES, dtype=jnp.int32) == chosen, K, counts)
    offset = jax.random.randint(key_offset, (ROW_TILES, K), -PANEL_TILES, 2 * PANEL_TILES)
    columns = jnp.mod(row_partition[:, None] * PANEL_TILES + offset, ROW_TILES)
    slot_index = jnp.arange(K, dtype=jnp.int32)[None, :]
    return jnp.where(slot_index < counts[:, None], columns, -1).astype(jnp.int32)


def draw_edge_weights(key, part):
    key = jax.random.fold_in(key, 37)
    key_present, key_lonely, key_values = jax.random.split(key, 3)
    full_shape = (ROW_TILES, K, 128, 128)
    present = jax.random.bernoulli(key_present, 0.5, full_shape)
    lonely = jax.random.bernoulli(key_lonely, 1.0 / 16.0, (ROW_TILES, 1, 128, 1))
    values = jnp.exp(jax.random.uniform(key_values, full_shape, jnp.float32, math.log(0.5), math.log(2.0)))
    weights = jnp.where(jnp.logical_and(present, jnp.logical_not(lonely)), values, 0.0)
    return weights.astype(jnp.bfloat16)


def block_levels(rng, shape, cuts, smallest, largest):
    def one(position, parts):
        draws = jax.random.uniform(jax.random.fold_in(jax.random.fold_in(rng, 6), position), (parts,), jnp.float32, smallest / len(cuts), largest / len(cuts))
        return jnp.repeat(jnp.exp(draws), shape[position] // parts).reshape((-1,) + (1,) * (len(shape) - position - 1))

    loudness = one(*cuts[0])
    for cut in cuts[1:]:
        loudness = loudness * one(*cut)
    return loudness


def normal_values(key, dims, scale, bound, cuts=(), kind=jnp.bfloat16):
    drawn = scale * jax.random.normal(key, dims, jnp.float32)
    if cuts:
        drawn = drawn * block_levels(key, dims, cuts, -0.22, 0.18)
    return jnp.clip(drawn, -bound, bound).astype(kind)


def setup_inputs(seed: int = 0) -> dict:
    arg_keys = jax.random.split(jax.random.key(seed), 11)
    features = normal_values(arg_keys[0], (F, TOKENS), 1.0, 6.0, ((0, 4), (1, 8)))
    w1_self = normal_values(arg_keys[1], (F, H), F ** -0.5, 0.5)
    w1_neigh = normal_values(arg_keys[2], (F, H), F ** -0.5, 0.5)
    b1 = normal_values(arg_keys[3], (H,), 0.5, 3.0, (), jnp.float32)
    w2_self = normal_values(arg_keys[4], (H, H), H ** -0.5, 0.375)
    w2_neigh = normal_values(arg_keys[5], (H, H), (H * 64) ** -0.5, 0.046875)
    b2 = normal_values(arg_keys[6], (H,), 0.5, 3.0, (), jnp.float32)
    col_tiles = draw_col_tiles(jax.random.fold_in(arg_keys[10], 71), 0)
    edge_weights = draw_edge_weights(jax.random.fold_in(arg_keys[10], 71), 0)
    cotangent = normal_values(arg_keys[9], (TOKENS, H), (TOKENS ** -0.5), 0.0625, ((0, 32),))
    return {"features": features, "w1_self": w1_self, "w1_neigh": w1_neigh, "b1": b1, "w2_self": w2_self, "w2_neigh": w2_neigh, "b2": b2, "col_tiles": col_tiles, "edge_weights": edge_weights, "cotangent": cotangent}


def aggregate_all(values, col_tiles, edge_weights):
    width = values.shape[1]
    tile_rows = values.reshape(ROW_TILES, 128, width)
    column_blocks = col_tiles.reshape(ROW_TILES // 8, 8, K)
    weight_blocks = edge_weights.reshape(ROW_TILES // 8, 8, K, 128, 128)

    def one_block(pair):
        columns, weights = pair
        occupied = columns >= 0
        clamped = jnp.where(occupied, columns, 0).astype(jnp.int32)
        adjacency = jnp.where(occupied[:, :, None, None], weights.astype(jnp.float32), jnp.float32(0.0))
        gathered = tile_rows[clamped].astype(jnp.float32)
        running = jnp.einsum('rkij,rkjc->ric', adjacency, gathered)
        degree = lax.optimization_barrier(jnp.sum(adjacency, axis=(1, 3)))
        return (running, degree)
    running, degree = lax.map(one_block, (column_blocks, weight_blocks))
    return (running.reshape(TOKENS, width), degree.reshape(TOKENS))

def reference(features, w1_self, w1_neigh, b1, w2_self, w2_neigh, b2, col_tiles, edge_weights, cotangent):
    node_rows = features.T
    self_one = jnp.dot(node_rows, w1_self, preferred_element_type=jnp.float32)
    summed_one, degree = aggregate_all(node_rows, col_tiles, edge_weights)
    neighbour_one = jnp.dot(summed_one, w1_neigh.astype(jnp.float32), precision=lax.Precision.HIGHEST)
    inv_root = lax.rsqrt(jnp.maximum(degree, jnp.float32(1.0)))[:, None]
    layer_one = jax.nn.relu(self_one + inv_root * neighbour_one + b1).astype(jnp.bfloat16)
    summed_two, unused = aggregate_all(layer_one, col_tiles, edge_weights)
    neighbour_two = (inv_root * summed_two).astype(jnp.bfloat16)
    embedding = (jnp.dot(layer_one, w2_self, preferred_element_type=jnp.float32) + jnp.dot(neighbour_two, w2_neigh, preferred_element_type=jnp.float32) + b2).astype(jnp.bfloat16)
    grad_w2_self = jnp.dot(layer_one.T, cotangent, preferred_element_type=jnp.float32)
    grad_w2_neigh = jnp.dot(neighbour_two.T, cotangent, preferred_element_type=jnp.float32)
    grad_b2 = lax.optimization_barrier(jnp.sum(cotangent.astype(jnp.float32), axis=0))
    return (embedding, grad_w2_self, grad_w2_neigh, grad_b2)
```

```python
import functools

import jax
import jax.numpy as jnp
from jax import lax
from jax.experimental import pallas as pl
from jax.experimental.pallas import tpu as pltpu
from jax.sharding import PartitionSpec as P

MESH = pl.DeviceIdType.MESH
GROUP = 8
VMEM_LIMIT = 56 * 1024 * 1024


def gather_kernel(n_dom, n_feat, pieces, x_ref, out_ref, own_sem, send_sem, recv_sem):
    dom, feat = lax.axis_index("dom"), lax.axis_index("feat")
    right, left = lax.rem(dom + 1, n_dom), lax.rem(dom + n_dom - 1, n_dom)
    above, below = lax.rem(feat + 1, n_feat), lax.rem(feat + n_feat - 1, n_feat)
    size = x_ref.shape[0] // pieces

    barrier = pltpu.get_barrier_semaphore()
    for where in ((left, feat), (right, feat), (dom, above), (dom, below)):
        pl.semaphore_signal(barrier, inc=1, device_id=where, device_id_type=MESH)
    pl.semaphore_wait(barrier, 4)

    def rows(piece):
        return pl.ds(piece * size, size)

    def copy(way, block, piece, own):
        slot, target = (
            (1, (dom, above)),
            (1, (dom, below)),
            (2, (left, feat)),
            (0, (right, feat)),
        )[way]
        source = x_ref if own else out_ref.at[1, block]
        return pltpu.make_async_remote_copy(
            src_ref=source.at[rows(piece)],
            dst_ref=out_ref.at[slot, block, rows(piece)],
            send_sem=send_sem.at[way, block, piece],
            recv_sem=recv_sem.at[slot, block, piece],
            device_id=target,
            device_id_type=MESH,
        )

    def arrival(slot, block, piece):
        part = out_ref.at[slot, block, rows(piece)]
        return pltpu.make_async_copy(part, part, recv_sem.at[slot, block, piece])

    keep = pltpu.make_async_copy(x_ref, out_ref.at[1, feat], own_sem)
    for piece in range(pieces):
        for way, there in ((0, feat < n_feat - 1), (1, feat > 0)):

            @pl.when(there)
            def _():
                copy(way, feat, piece, True).start()

        copy(2, feat, piece, True).start()
        copy(3, feat, piece, True).start()
    keep.start()

    for step in range(1, n_feat):
        for piece in range(pieces):
            for way, block, there, onward in (
                (0, feat - step, feat >= step, feat < n_feat - 1),
                (1, feat + step, feat + step < n_feat, feat > 0),
            ):

                @pl.when(there)
                def _():
                    arrival(1, block, piece).wait()

                    @pl.when(onward)
                    def _():
                        copy(way, block, piece, False).start()

                    copy(2, block, piece, False).start()
                    copy(3, block, piece, False).start()

    keep.wait()
    for piece in range(pieces):
        for way, there in ((0, feat < n_feat - 1), (1, feat > 0)):

            @pl.when(there)
            def _():
                copy(way, feat, piece, True).wait_send()

        copy(2, feat, piece, True).wait_send()
        copy(3, feat, piece, True).wait_send()
        for step in range(1, n_feat):
            for way, block, there, onward in (
                (0, feat - step, feat >= step, feat < n_feat - 1),
                (1, feat + step, feat + step < n_feat, feat > 0),
            ):

                @pl.when(there)
                def _():
                    @pl.when(onward)
                    def _():
                        copy(way, block, piece, False).wait_send()

                    copy(2, block, piece, False).wait_send()
                    copy(3, block, piece, False).wait_send()

        for block in range(n_feat):
            arrival(0, block, piece).wait()
            arrival(2, block, piece).wait()


def gather(block, n_dom, n_feat, pieces, collective_id, name):
    return pl.pallas_call(
        functools.partial(gather_kernel, n_dom, n_feat, pieces),
        out_shape=jax.ShapeDtypeStruct((3, n_feat) + block.shape, block.dtype),
        in_specs=[pl.BlockSpec(memory_space=pl.ANY)],
        out_specs=pl.BlockSpec(memory_space=pl.ANY),
        scratch_shapes=[
            pltpu.SemaphoreType.DMA,
            pltpu.SemaphoreType.DMA((4, n_feat, pieces)),
            pltpu.SemaphoreType.DMA((3, n_feat, pieces)),
        ],
        compiler_params=pltpu.CompilerParams(
            collective_id=collective_id, has_side_effects=True
        ),
        name=name,
    )(block)


def live_group(edge_ref, tile, first, count):
    parts = []
    for lane in range(GROUP):
        weights = edge_ref[tile, first + lane]
        parts.append(jnp.where(first + lane < count, weights, jnp.zeros_like(weights)))
    return parts


def first_kernel(
    panel_tiles, where_ref, count_ref, feat_ref, panel_ref, edge_ref, ws_ref, wn_ref, b_ref,
    layer_ref, root_ref,
):
    tile = pl.program_id(0)
    count = count_ref[tile]

    def one_group(turn, carry):
        total, degree = carry
        first = turn * GROUP
        parts = live_group(edge_ref, 0, first, count)
        picked = []
        for lane in range(GROUP):
            at = where_ref[tile, first + lane]
            column = pl.multiple_of(lax.rem(at, panel_tiles) * 128, 128)
            picked.append(panel_ref[lax.div(at, panel_tiles), :, pl.ds(column, 128)])
        total += lax.dot_general(
            jnp.concatenate(parts, axis=1),
            jnp.concatenate(picked, axis=1),
            (((1,), (1,)), ((), ())),
            preferred_element_type=jnp.float32,
        )
        for part in parts:
            degree += part.astype(jnp.float32)
        return total, degree

    zeros = jnp.zeros((128, 128), jnp.float32)
    summed, degree = lax.fori_loop(0, pl.cdiv(count, GROUP), one_group, (zeros, zeros))
    degree = jnp.sum(degree, axis=1, keepdims=True)
    inv_root = lax.rsqrt(jnp.maximum(degree, 1.0))
    neighbour = jnp.zeros(layer_ref.shape, jnp.float32)
    rest = summed
    for _ in range(3):
        piece = rest.astype(jnp.bfloat16)
        rest = rest - piece.astype(jnp.float32)
        neighbour += jnp.dot(piece, wn_ref[...], preferred_element_type=jnp.float32)
    own = pl.multiple_of((feat_ref[0] * pl.num_programs(0) + tile) * 128, 128)
    self_one = lax.dot_general(
        panel_ref[1, :, pl.ds(own, 128)],
        ws_ref[...],
        (((0,), (0,)), ((), ())),
        preferred_element_type=jnp.float32,
    )
    layer = self_one + inv_root * neighbour + b_ref[...]
    layer_ref[...] = jnp.maximum(layer, 0.0).astype(layer_ref.dtype)
    root_ref[...] = jnp.broadcast_to(inv_root, root_ref.shape)


def second_kernel(
    where_ref, count_ref, panel_ref, edge_ref, layer_ref, root_ref, cot_ref, ws_ref, wn_ref,
    b_ref, emb_ref, grad_ref, bias_ref,
):
    tile = pl.program_id(0)
    count = count_ref[tile]
    hidden = layer_ref.shape[1]

    def one_group(turn, total):
        first = turn * GROUP
        parts = live_group(edge_ref, 0, first, count)
        picked = [panel_ref[where_ref[tile, first + lane]] for lane in range(GROUP)]
        return total + jnp.dot(
            jnp.concatenate(parts, axis=1),
            jnp.concatenate(picked, axis=0),
            preferred_element_type=jnp.float32,
        )

    zeros = jnp.zeros((128, hidden), jnp.float32)
    summed = lax.fori_loop(0, pl.cdiv(count, GROUP), one_group, zeros)
    neighbour = (root_ref[:, :1] * summed).astype(jnp.bfloat16)
    layer = layer_ref[...]
    embedding = (
        jnp.dot(layer, ws_ref[...], preferred_element_type=jnp.float32)
        + jnp.dot(neighbour, wn_ref[...], preferred_element_type=jnp.float32)
        + b_ref[...]
    )
    emb_ref[...] = embedding.astype(emb_ref.dtype)
    cotangent = cot_ref[...]

    @pl.when(tile == 0)
    def _():
        grad_ref[...] = jnp.zeros_like(grad_ref)
        bias_ref[...] = jnp.zeros_like(bias_ref)

    grad_ref[...] += lax.dot_general(
        jnp.concatenate([layer, neighbour], axis=1),
        cotangent,
        (((0,), (0,)), ((), ())),
        preferred_element_type=jnp.float32,
    )
    bias_ref[...] += jnp.sum(
        cotangent.astype(jnp.float32).reshape(16, 8, cotangent.shape[1]), axis=0
    )


def reduce_kernel(
    n_dom, n_feat, g_ref, b_ref, out_ref, bias_ref,
    by_dom, bias_dom, by_feat, bias_feat, send_sem, recv_sem,
):
    dom, feat = lax.axis_index("dom"), lax.axis_index("feat")
    share = g_ref.shape[0] // n_dom

    def dom_at(step):
        return lax.rem(dom + step, n_dom)

    def feat_at(step):
        return lax.rem(feat + step, n_feat)

    def rows(index):
        return pl.ds(pl.multiple_of(index * share, share), share)

    def copy(kind, source, target, step, device_id):
        return pltpu.make_async_remote_copy(
            src_ref=source,
            dst_ref=target,
            send_sem=send_sem.at[kind, step],
            recv_sem=recv_sem.at[kind, step],
            device_id=device_id,
            device_id_type=MESH,
        )

    barrier = pltpu.get_barrier_semaphore()
    for step in range(1, n_dom):
        pl.semaphore_signal(
            barrier, inc=1, device_id=(dom_at(step), feat), device_id_type=MESH
        )
    for step in range(1, n_feat):
        pl.semaphore_signal(
            barrier, inc=1, device_id=(dom, feat_at(step)), device_id_type=MESH
        )
    pl.semaphore_wait(barrier, n_dom + n_feat - 2)

    scatter = []
    for step in range(1, n_dom):
        to = (dom_at(step), feat)
        scatter.append(copy(0, g_ref.at[rows(dom_at(step))], by_dom.at[dom], step, to))
        scatter.append(copy(1, b_ref, bias_dom.at[dom], step, to))
    for each in scatter:
        each.start()
    by_dom[dom] = g_ref[rows(dom), :]
    bias_dom[dom] = b_ref[...]
    for each in scatter:
        each.wait()
    by_feat[feat] = functools.reduce(lambda a, b: a + b, [by_dom[i] for i in range(n_dom)])
    bias_feat[feat] = functools.reduce(
        lambda a, b: a + b, [bias_dom[i] for i in range(n_dom)]
    )

    across = []
    for step in range(1, n_feat):
        to = (dom, feat_at(step))
        across.append(copy(2, by_feat.at[feat], by_feat.at[feat], step, to))
        across.append(copy(3, bias_feat.at[feat], bias_feat.at[feat], step, to))
    for each in across:
        each.start()
    for each in across:
        each.wait()
    out_ref[rows(dom), :] = functools.reduce(
        lambda a, b: a + b, [by_feat[i] for i in range(n_feat)]
    )
    bias_ref[...] = functools.reduce(lambda a, b: a + b, [bias_feat[i] for i in range(n_feat)])

    spread = [
        copy(4, out_ref.at[rows(dom)], out_ref.at[rows(dom)], step, (dom_at(step), feat))
        for step in range(1, n_dom)
    ]
    for each in spread:
        each.start()
    for each in spread:
        each.wait()


def reduce_all(grads, bias, n_dom, n_feat):
    share = grads.shape[0] // n_dom
    width = grads.shape[1]
    steps = max(n_dom, n_feat)
    whole = pl.BlockSpec(memory_space=pltpu.VMEM)
    return pl.pallas_call(
        functools.partial(reduce_kernel, n_dom, n_feat),
        out_shape=(
            jax.ShapeDtypeStruct(grads.shape, jnp.float32),
            jax.ShapeDtypeStruct(bias.shape, jnp.float32),
        ),
        in_specs=[whole] * 2,
        out_specs=(whole, whole),
        scratch_shapes=[
            pltpu.VMEM((n_dom, share, width), jnp.float32),
            pltpu.VMEM((n_dom,) + bias.shape, jnp.float32),
            pltpu.VMEM((n_feat, share, width), jnp.float32),
            pltpu.VMEM((n_feat,) + bias.shape, jnp.float32),
            pltpu.SemaphoreType.DMA((5, steps)),
            pltpu.SemaphoreType.DMA((5, steps)),
        ],
        compiler_params=pltpu.CompilerParams(
            collective_id=2, has_side_effects=True, vmem_limit_bytes=VMEM_LIMIT
        ),
        name="reduce_all",
    )(grads, bias)


def on_device(
    features, w1_self, w1_neigh, b1, w2_self, w2_neigh, b2, col_tiles, edge_weights, cotangent
):
    n_feat = lax.axis_size("feat")
    n_dom = lax.axis_size("dom")
    row_tiles, slots = col_tiles.shape
    panel_tiles = row_tiles * n_feat
    all_tiles = panel_tiles * n_dom
    inputs, hidden = w1_self.shape
    occupied = col_tiles >= 0
    relative = jnp.mod(col_tiles - (lax.axis_index("dom") - 1) * panel_tiles, all_tiles)
    relative = jnp.where(occupied, relative, 0)
    counts = jnp.sum(occupied.astype(jnp.int32), axis=1)
    feat = jnp.full((1,), lax.axis_index("feat"), jnp.int32)

    def fixed(*shape):
        return pl.BlockSpec(
            shape, lambda r, *_: (0,) * len(shape), pipeline_mode=pl.Buffered(1)
        )

    def by_tile(width):
        return pl.BlockSpec((128, width), lambda r, *_: (r, 0))

    edges = pl.BlockSpec((1, slots, 128, 128), lambda r, *_: (r, 0, 0, 0))
    rows = row_tiles * 128

    panel_one = gather(features, n_dom, n_feat, 2, 0, "gather_features")
    panel_one = panel_one.reshape(3, inputs, panel_tiles * 128)
    layer_one, inv_root = pl.pallas_call(
        functools.partial(first_kernel, panel_tiles),
        grid_spec=pltpu.PrefetchScalarGridSpec(
            num_scalar_prefetch=3,
            grid=(row_tiles,),
            in_specs=[
                fixed(3, inputs, panel_tiles * 128),
                edges,
                fixed(inputs, hidden),
                fixed(inputs, hidden),
                fixed(1, hidden),
            ],
            out_specs=(by_tile(hidden), by_tile(128)),
        ),
        out_shape=(
            jax.ShapeDtypeStruct((rows, hidden), jnp.bfloat16),
            jax.ShapeDtypeStruct((rows, 128), jnp.float32),
        ),
        compiler_params=pltpu.CompilerParams(vmem_limit_bytes=VMEM_LIMIT),
        name="first_layer",
    )(relative, counts, feat, panel_one, edge_weights, w1_self, w1_neigh, b1[None])

    panel_two = gather(layer_one, n_dom, n_feat, 4, 1, "gather_layer_one")
    panel_two = panel_two.reshape(3 * panel_tiles, 128, hidden)
    embedding, grads, bias = pl.pallas_call(
        second_kernel,
        grid_spec=pltpu.PrefetchScalarGridSpec(
            num_scalar_prefetch=2,
            grid=(row_tiles,),
            in_specs=[
                fixed(3 * panel_tiles, 128, hidden),
                edges,
                by_tile(hidden),
                by_tile(128),
                by_tile(hidden),
                fixed(hidden, hidden),
                fixed(hidden, hidden),
                fixed(1, hidden),
            ],
            out_specs=(
                by_tile(hidden),
                pl.BlockSpec((2 * hidden, hidden), lambda r, *_: (0, 0)),
                pl.BlockSpec((8, hidden), lambda r, *_: (0, 0)),
            ),
        ),
        out_shape=(
            jax.ShapeDtypeStruct((rows, hidden), jnp.bfloat16),
            jax.ShapeDtypeStruct((2 * hidden, hidden), jnp.float32),
            jax.ShapeDtypeStruct((8, hidden), jnp.float32),
        ),
        compiler_params=pltpu.CompilerParams(vmem_limit_bytes=VMEM_LIMIT),
        name="second_layer",
    )(
        relative, counts, panel_two, edge_weights, layer_one, inv_root, cotangent,
        w2_self, w2_neigh, b2[None],
    )
    grads, bias = reduce_all(grads, bias, n_dom, n_feat)
    return (embedding, grads[:hidden], grads[hidden:], jnp.sum(bias, axis=0))


def solution(mesh):
    placed = (
        P("feat", "dom"),
        P(),
        P(),
        P(),
        P(),
        P(),
        P(),
        P(("dom", "feat"), None),
        P(("dom", "feat"), None, None, None),
        P(("dom", "feat"), None),
    )
    return jax.shard_map(
        on_device,
        mesh=mesh,
        in_specs=placed,
        out_specs=(P(("dom", "feat"), None), P(), P(), P()),
        check_vma=False,
    )
```

```python
import functools

import jax
import jax.numpy as jnp
from jax import lax
from jax.experimental import pallas as pl
from jax.experimental.pallas import tpu as pltpu
from jax.sharding import PartitionSpec as P

MESH = pl.DeviceIdType.MESH
GROUP = 8
PIECES_ONE = 2
PIECES_TWO = 4
VMEM_LIMIT = 56 * 1024 * 1024


def live_group(edge_ref, tile, first, count):
    parts = []
    for lane in range(GROUP):
        weights = edge_ref[tile, first + lane]
        parts.append(jnp.where(first + lane < count, weights, jnp.zeros_like(weights)))
    return parts


def first_kernel(
    n_dom, n_feat, x_ref, where_ref, live_ref, edge_hbm, ws_ref, wn_ref, b_ref,
    out_ref, root_ref,
    panel, tiles_ref, edge_ref, layer_ref, own_sem, edge_sem, send_one, recv_one, send_two, recv_two,
):
    dom, feat = lax.axis_index("dom"), lax.axis_index("feat")
    right, left = lax.rem(dom + 1, n_dom), lax.rem(dom + n_dom - 1, n_dom)
    above, below = lax.rem(feat + 1, n_feat), lax.rem(feat + n_feat - 1, n_feat)
    row_tiles, slots = edge_ref.shape[:2]
    step_tiles = row_tiles // PIECES_TWO

    def edge_copy(piece):
        part = pl.ds(piece * step_tiles, step_tiles)
        return pltpu.make_async_copy(edge_hbm.at[part], edge_ref.at[part], edge_sem.at[piece])

    for piece in range(PIECES_TWO):
        edge_copy(piece).start()

    barrier = pltpu.get_barrier_semaphore()
    for where in ((left, feat), (right, feat), (dom, above), (dom, below)):
        pl.semaphore_signal(barrier, inc=1, device_id=where, device_id_type=MESH)
    pl.semaphore_wait(barrier, 4)

    def gather(block_ref, held_ref, pieces, send_sem, recv_sem):
        size = block_ref.shape[0] // pieces

        def rows(piece):
            return pl.ds(piece * size, size)

        def copy(way, block, piece, own):
            slot, target = (
                (1, (dom, above)),
                (1, (dom, below)),
                (2, (left, feat)),
                (0, (right, feat)),
            )[way]
            source = block_ref if own else held_ref.at[1, block]
            return pltpu.make_async_remote_copy(
                src_ref=source.at[rows(piece)],
                dst_ref=held_ref.at[slot, block, rows(piece)],
                send_sem=send_sem.at[way, block, piece],
                recv_sem=recv_sem.at[slot, block, piece],
                device_id=target,
                device_id_type=MESH,
            )

        def arrival(slot, block, piece):
            part = held_ref.at[slot, block, rows(piece)]
            return pltpu.make_async_copy(part, part, recv_sem.at[slot, block, piece])

        def send_own(piece):
            for way, there in ((0, feat < n_feat - 1), (1, feat > 0)):

                @pl.when(there)
                def _():
                    copy(way, feat, piece, True).start()

            copy(2, feat, piece, True).start()
            copy(3, feat, piece, True).start()

        def streams(step):
            return (
                (0, feat - step, feat >= step, feat < n_feat - 1),
                (1, feat + step, feat + step < n_feat, feat > 0),
            )

        def forward():
            for step in range(1, n_feat):
                for piece in range(pieces):
                    for way, block, there, onward in streams(step):

                        @pl.when(there)
                        def _():
                            arrival(1, block, piece).wait()

                            @pl.when(onward)
                            def _():
                                copy(way, block, piece, False).start()

                            copy(2, block, piece, False).start()
                            copy(3, block, piece, False).start()

        def finish_sends():
            for piece in range(pieces):
                for way, there in ((0, feat < n_feat - 1), (1, feat > 0)):

                    @pl.when(there)
                    def _():
                        copy(way, feat, piece, True).wait_send()

                copy(2, feat, piece, True).wait_send()
                copy(3, feat, piece, True).wait_send()
                for step in range(1, n_feat):
                    for way, block, there, onward in streams(step):

                        @pl.when(there)
                        def _():
                            @pl.when(onward)
                            def _():
                                copy(way, block, piece, False).wait_send()

                            copy(2, block, piece, False).wait_send()
                            copy(3, block, piece, False).wait_send()

        def arrive():
            for piece in range(pieces):
                for block in range(n_feat):
                    arrival(0, block, piece).wait()
                    arrival(2, block, piece).wait()

        return send_own, forward, finish_sends, arrive

    send_own, forward, finish_one, arrive = gather(x_ref, panel, PIECES_ONE, send_one, recv_one)
    keep = pltpu.make_async_copy(x_ref, panel.at[1, feat], own_sem)
    for piece in range(PIECES_ONE):
        send_own(piece)
    keep.start()
    forward()
    keep.wait()
    arrive()

    width = panel.shape[1] * panel.shape[2]
    hidden = layer_ref.shape[1]
    panel_tiles = panel.shape[3] // 128

    tiles_ref[3 * panel_tiles] = jnp.zeros((width, 128), tiles_ref.dtype)

    @pl.loop(0, panel_tiles)
    def _(at):
        column = pl.multiple_of(at * 128, 128)
        for slot in range(3):
            cells = panel[slot, :, :, pl.ds(column, 128)]
            tiles_ref[slot * panel_tiles + at] = cells.reshape(width, 128)

    def two_tiles(pair):
        def one_group(turn, carry):
            done = []
            for half in range(2):
                total, degree = carry[half]
                tile = pair * 2 + half
                first = turn * GROUP
                parts = [edge_ref[tile, first + lane] for lane in range(GROUP)]
                picked = [tiles_ref[where_ref[tile, first + lane]] for lane in range(GROUP)]
                total += lax.dot_general(
                    jnp.concatenate(parts, axis=1),
                    jnp.concatenate(picked, axis=1),
                    (((1,), (1,)), ((), ())),
                    preferred_element_type=jnp.float32,
                )
                for lane, part in enumerate(parts):
                    live = live_ref[pl.ds(tile * slots + first + lane, 1), :]
                    degree += part.astype(jnp.float32) * live
                done.append((total, degree))
            return tuple(done)

        zeros = (jnp.zeros((128, width), jnp.float32), jnp.zeros((128, 128), jnp.float32))
        sums = lax.fori_loop(0, slots // GROUP, one_group, (zeros, zeros))
        rest = jnp.concatenate([total for total, _ in sums], axis=0)
        degree = jnp.sum(
            jnp.concatenate([each for _, each in sums], axis=0), axis=1, keepdims=True
        )
        inv_root = lax.rsqrt(jnp.maximum(degree, 1.0))
        neighbour = jnp.zeros((256, hidden), jnp.float32)
        for _ in range(3):
            piece = rest.astype(jnp.bfloat16)
            rest = rest - piece.astype(jnp.float32)
            neighbour += jnp.dot(piece, wn_ref[...], preferred_element_type=jnp.float32)
        own = pl.multiple_of((feat * row_tiles + pair * 2) * 128, 256)
        self_one = lax.dot_general(
            panel[1, :, :, pl.ds(own, 256)].reshape(width, 256),
            ws_ref[...],
            (((0,), (0,)), ((), ())),
            preferred_element_type=jnp.float32,
        )
        layer = jnp.maximum(self_one + inv_root * neighbour + b_ref[...], 0.0)
        rows = pl.ds(pl.multiple_of(pair * 256, 256), 256)
        layer_ref[rows, :] = layer.astype(layer_ref.dtype)
        root_ref[rows, :] = jnp.broadcast_to(inv_root, (256, 128))

    send_own, forward, finish_two, arrive = gather(
        layer_ref, out_ref, PIECES_TWO, send_two, recv_two
    )
    pairs = step_tiles // 2
    for piece in range(PIECES_TWO):
        edge_copy(piece).wait()
        pl.loop(piece * pairs, (piece + 1) * pairs)(two_tiles)
        send_own(piece)
    keep = pltpu.make_async_copy(layer_ref, out_ref.at[1, feat], own_sem)
    keep.start()
    forward()
    keep.wait()
    finish_one()
    finish_two()
    arrive()


def second_kernel(
    where_ref, count_ref, first_ref, panel_ref, edge_ref, root_ref, cot_ref, ws_ref,
    wn_ref, b_ref, emb_ref, grad_ref, bias_ref,
):
    step = pl.program_id(0)
    hidden = emb_ref.shape[1]
    sums, own = [], []
    for half in range(2):
        tile = step * 2 + half
        count = count_ref[tile]

        def one_group(turn, total):
            first = turn * GROUP
            parts = live_group(edge_ref, half, first, count)
            picked = [panel_ref[where_ref[tile, first + lane]] for lane in range(GROUP)]
            return total + jnp.dot(
                jnp.concatenate(parts, axis=1),
                jnp.concatenate(picked, axis=0),
                preferred_element_type=jnp.float32,
            )

        zeros = jnp.zeros((128, hidden), jnp.float32)
        sums.append(lax.fori_loop(0, pl.cdiv(count, GROUP), one_group, zeros))
        own.append(panel_ref[first_ref[0] + tile])
    summed = jnp.concatenate(sums, axis=0)
    neighbour = (root_ref[:, :1] * summed).astype(jnp.bfloat16)
    layer = jnp.concatenate(own, axis=0)
    embedding = (
        jnp.dot(layer, ws_ref[...], preferred_element_type=jnp.float32)
        + jnp.dot(neighbour, wn_ref[...], preferred_element_type=jnp.float32)
        + b_ref[...]
    )
    emb_ref[...] = embedding.astype(emb_ref.dtype)
    cotangent = cot_ref[...]

    @pl.when(step == 0)
    def _():
        grad_ref[...] = jnp.zeros_like(grad_ref)
        bias_ref[...] = jnp.zeros_like(bias_ref)

    grad_ref[...] += lax.dot_general(
        jnp.concatenate([layer, neighbour], axis=1),
        cotangent,
        (((0,), (0,)), ((), ())),
        preferred_element_type=jnp.float32,
    )
    bias_ref[...] += jnp.sum(
        cotangent.astype(jnp.float32).reshape(-1, 8, cotangent.shape[1]), axis=0
    )


def reduce_kernel(
    n_dom, n_feat, g_ref, b_ref, out_ref, bias_ref,
    by_dom, bias_dom, by_feat, bias_feat, send_sem, recv_sem,
):
    dom, feat = lax.axis_index("dom"), lax.axis_index("feat")
    share = g_ref.shape[0] // n_dom

    def dom_at(step):
        return lax.rem(dom + step, n_dom)

    def feat_at(step):
        return lax.rem(feat + step, n_feat)

    def rows(index):
        return pl.ds(pl.multiple_of(index * share, share), share)

    def copy(kind, source, target, step, device_id):
        return pltpu.make_async_remote_copy(
            src_ref=source,
            dst_ref=target,
            send_sem=send_sem.at[kind, step],
            recv_sem=recv_sem.at[kind, step],
            device_id=device_id,
            device_id_type=MESH,
        )

    barrier = pltpu.get_barrier_semaphore()
    for step in range(1, n_dom):
        pl.semaphore_signal(
            barrier, inc=1, device_id=(dom_at(step), feat), device_id_type=MESH
        )
    for step in range(1, n_feat):
        pl.semaphore_signal(
            barrier, inc=1, device_id=(dom, feat_at(step)), device_id_type=MESH
        )
    pl.semaphore_wait(barrier, n_dom + n_feat - 2)

    scatter = []
    for step in range(1, n_dom):
        to = (dom_at(step), feat)
        scatter.append(copy(0, g_ref.at[rows(dom_at(step))], by_dom.at[dom], step, to))
        scatter.append(copy(1, b_ref, bias_dom.at[dom], step, to))
    for each in scatter:
        each.start()
    by_dom[dom] = g_ref[rows(dom), :]
    bias_dom[dom] = b_ref[...]
    for each in scatter:
        each.wait()
    by_feat[feat] = functools.reduce(lambda a, b: a + b, [by_dom[i] for i in range(n_dom)])
    bias_feat[feat] = functools.reduce(
        lambda a, b: a + b, [bias_dom[i] for i in range(n_dom)]
    )

    across = []
    for step in range(1, n_feat):
        to = (dom, feat_at(step))
        across.append(copy(2, by_feat.at[feat], by_feat.at[feat], step, to))
        across.append(copy(3, bias_feat.at[feat], bias_feat.at[feat], step, to))
    for each in across:
        each.start()
    for each in across:
        each.wait()
    out_ref[rows(dom), :] = functools.reduce(
        lambda a, b: a + b, [by_feat[i] for i in range(n_feat)]
    )
    bias_ref[...] = functools.reduce(lambda a, b: a + b, [bias_feat[i] for i in range(n_feat)])

    spread = [
        copy(4, out_ref.at[rows(dom)], out_ref.at[rows(dom)], step, (dom_at(step), feat))
        for step in range(1, n_dom)
    ]
    for each in spread:
        each.start()
    for each in spread:
        each.wait()


def reduce_all(grads, bias, n_dom, n_feat):
    share = grads.shape[0] // n_dom
    width = grads.shape[1]
    steps = max(n_dom, n_feat)
    whole = pl.BlockSpec(memory_space=pltpu.VMEM)
    return pl.pallas_call(
        functools.partial(reduce_kernel, n_dom, n_feat),
        out_shape=(
            jax.ShapeDtypeStruct(grads.shape, jnp.float32),
            jax.ShapeDtypeStruct(bias.shape, jnp.float32),
        ),
        in_specs=[whole] * 2,
        out_specs=(whole, whole),
        scratch_shapes=[
            pltpu.VMEM((n_dom, share, width), jnp.float32),
            pltpu.VMEM((n_dom,) + bias.shape, jnp.float32),
            pltpu.VMEM((n_feat, share, width), jnp.float32),
            pltpu.VMEM((n_feat,) + bias.shape, jnp.float32),
            pltpu.SemaphoreType.DMA((5, steps)),
            pltpu.SemaphoreType.DMA((5, steps)),
        ],
        compiler_params=pltpu.CompilerParams(
            collective_id=2, has_side_effects=True, vmem_limit_bytes=VMEM_LIMIT
        ),
        name="reduce_all",
    )(grads, bias)


def on_device(
    features, w1_self, w1_neigh, b1, w2_self, w2_neigh, b2, col_tiles, edge_weights, cotangent
):
    n_feat = lax.axis_size("feat")
    n_dom = lax.axis_size("dom")
    row_tiles, slots = col_tiles.shape
    panel_tiles = row_tiles * n_feat
    all_tiles = panel_tiles * n_dom
    hidden = w1_self.shape[1]
    occupied = col_tiles >= 0
    relative = jnp.mod(col_tiles - (lax.axis_index("dom") - 1) * panel_tiles, all_tiles)
    relative = jnp.where(occupied, relative, 3 * panel_tiles)
    live = jnp.broadcast_to(
        occupied.astype(jnp.float32).reshape(row_tiles * slots, 1), (row_tiles * slots, 128)
    )
    counts = jnp.sum(occupied.astype(jnp.int32), axis=1)
    first_own = jnp.full(
        (1,), panel_tiles + lax.axis_index("feat") * row_tiles, jnp.int32
    )
    rows = row_tiles * 128
    whole = pl.BlockSpec(memory_space=pltpu.VMEM)
    scalars = pl.BlockSpec(memory_space=pltpu.SMEM)
    anywhere = pl.BlockSpec(memory_space=pl.ANY)
    dma = pltpu.SemaphoreType.DMA

    panel_two, inv_root = pl.pallas_call(
        functools.partial(first_kernel, n_dom, n_feat),
        out_shape=(
            jax.ShapeDtypeStruct((3, n_feat, rows, hidden), jnp.bfloat16),
            jax.ShapeDtypeStruct((rows, 128), jnp.float32),
        ),
        in_specs=[anywhere, scalars, whole, anywhere, whole, whole, whole],
        out_specs=(anywhere, whole),
        scratch_shapes=[
            pltpu.VMEM((3, n_feat) + features.shape, jnp.bfloat16),
            pltpu.VMEM((3 * panel_tiles + 1, w1_self.shape[0], 128), jnp.bfloat16),
            pltpu.VMEM(edge_weights.shape, jnp.bfloat16),
            pltpu.VMEM((rows, hidden), jnp.bfloat16),
            dma,
            dma((PIECES_TWO,)),
            dma((4, n_feat, PIECES_ONE)),
            dma((3, n_feat, PIECES_ONE)),
            dma((4, n_feat, PIECES_TWO)),
            dma((3, n_feat, PIECES_TWO)),
        ],
        compiler_params=pltpu.CompilerParams(
            collective_id=0, has_side_effects=True, vmem_limit_bytes=VMEM_LIMIT
        ),
        name="first_layer",
    )(
        features,
        relative,
        live,
        edge_weights,
        w1_self,
        w1_neigh,
        b1[None],
    )

    def fixed(*shape):
        return pl.BlockSpec(
            shape, lambda r, *_: (0,) * len(shape), pipeline_mode=pl.Buffered(1)
        )

    def by_step(width):
        return pl.BlockSpec((256, width), lambda r, *_: (r, 0))

    panel_two = panel_two.reshape(3 * panel_tiles, 128, hidden)
    embedding, grads, bias = pl.pallas_call(
        second_kernel,
        grid_spec=pltpu.PrefetchScalarGridSpec(
            num_scalar_prefetch=3,
            grid=(row_tiles // 2,),
            in_specs=[
                fixed(3 * panel_tiles, 128, hidden),
                pl.BlockSpec((2, slots, 128, 128), lambda r, *_: (r, 0, 0, 0)),
                by_step(128),
                by_step(hidden),
                fixed(hidden, hidden),
                fixed(hidden, hidden),
                fixed(1, hidden),
            ],
            out_specs=(
                by_step(hidden),
                pl.BlockSpec((2 * hidden, hidden), lambda r, *_: (0, 0)),
                pl.BlockSpec((8, hidden), lambda r, *_: (0, 0)),
            ),
        ),
        out_shape=(
            jax.ShapeDtypeStruct((rows, hidden), jnp.bfloat16),
            jax.ShapeDtypeStruct((2 * hidden, hidden), jnp.float32),
            jax.ShapeDtypeStruct((8, hidden), jnp.float32),
        ),
        compiler_params=pltpu.CompilerParams(vmem_limit_bytes=VMEM_LIMIT),
        name="second_layer",
    )(
        jnp.where(occupied, relative, 0), counts, first_own, panel_two, edge_weights, inv_root, cotangent,
        w2_self, w2_neigh, b2[None],
    )
    grads, bias = reduce_all(grads, bias, n_dom, n_feat)
    return (embedding, grads[:hidden], grads[hidden:], jnp.sum(bias, axis=0))


def solution(mesh):
    placed = (
        P("feat", "dom"),
        P(),
        P(),
        P(),
        P(),
        P(),
        P(),
        P(("dom", "feat"), None),
        P(("dom", "feat"), None, None, None),
        P(("dom", "feat"), None),
    )
    return jax.shard_map(
        on_device,
        mesh=mesh,
        in_specs=placed,
        out_specs=(P(("dom", "feat"), None), P(), P(), P()),
        check_vma=False,
    )
```

```python
import functools

import jax
import jax.numpy as jnp
from jax import lax
from jax.experimental import pallas as pl
from jax.experimental.pallas import tpu as pltpu
from jax.sharding import PartitionSpec as P

MESH = pl.DeviceIdType.MESH
GROUP = 8
PIECES_ONE = 2
PIECES_TWO = 4
VMEM_LIMIT = 56 * 1024 * 1024


def live_group(edge_ref, tile, first, count):
    parts = []
    for lane in range(GROUP):
        weights = edge_ref[tile, first + lane]
        parts.append(jnp.where(first + lane < count, weights, jnp.zeros_like(weights)))
    return parts


def first_kernel(
    n_dom, n_feat, x_ref, where_ref, live_ref, edge_hbm, ws_ref, wn_ref, b_ref,
    out_ref, root_ref,
    panel, tiles_ref, edge_ref, layer_ref, own_sem, edge_sem, send_one, recv_one, send_two, recv_two,
):
    dom, feat = lax.axis_index("dom"), lax.axis_index("feat")
    right, left = lax.rem(dom + 1, n_dom), lax.rem(dom + n_dom - 1, n_dom)
    above, below = lax.rem(feat + 1, n_feat), lax.rem(feat + n_feat - 1, n_feat)
    row_tiles, slots = edge_ref.shape[:2]
    step_tiles = row_tiles // PIECES_TWO

    def edge_copy(piece):
        part = pl.ds(piece * step_tiles, step_tiles)
        return pltpu.make_async_copy(edge_hbm.at[part], edge_ref.at[part], edge_sem.at[piece])

    for piece in range(PIECES_TWO):
        edge_copy(piece).start()

    barrier = pltpu.get_barrier_semaphore()
    for where in ((left, feat), (right, feat), (dom, above), (dom, below)):
        pl.semaphore_signal(barrier, inc=1, device_id=where, device_id_type=MESH)
    pl.semaphore_wait(barrier, 4)

    def gather(block_ref, held_ref, pieces, send_sem, recv_sem):
        size = block_ref.shape[0] // pieces

        def rows(piece):
            return pl.ds(piece * size, size)

        def copy(way, block, piece, own):
            slot, target = (
                (1, (dom, above)),
                (1, (dom, below)),
                (2, (left, feat)),
                (0, (right, feat)),
            )[way]
            source = block_ref if own else held_ref.at[1, block]
            return pltpu.make_async_remote_copy(
                src_ref=source.at[rows(piece)],
                dst_ref=held_ref.at[slot, block, rows(piece)],
                send_sem=send_sem.at[way, block, piece],
                recv_sem=recv_sem.at[slot, block, piece],
                device_id=target,
                device_id_type=MESH,
            )

        half = pieces // 2 if n_feat >= 4 else 0
        even = lax.rem(dom, 2) == 0
        far = 2 * lax.rem(dom, 2)
        relays = (
            (0, 0, above, (feat == 0) | (feat == n_feat - 2)),
            (1, n_feat - 1, below, (feat == 1) | (feat == n_feat - 1)),
        )

        def relayed(block):
            return (((feat == 0) | (feat == n_feat - 2)) & (block == n_feat - 1)) | (
                ((feat == 1) | (feat == n_feat - 1)) & (block == 0)
            )

        def across(block, piece, own, act):
            for way, outer in ((2, even), (3, jnp.logical_not(even))):
                if piece < half:
                    pl.when(jnp.logical_not(outer & relayed(block)))(
                        lambda way=way: act(copy(way, block, piece, own))
                    )
                else:
                    act(copy(way, block, piece, own))

        def relay_copy(block, target, piece):
            part = held_ref.at[far, block, rows(piece)]
            return pltpu.make_async_remote_copy(
                src_ref=part,
                dst_ref=part,
                send_sem=send_sem.at[4, block, piece],
                recv_sem=recv_sem.at[far, block, piece],
                device_id=(dom, target),
                device_id_type=MESH,
            )

        def relay():
            for piece in range(half):
                for _, block, target, there in relays:

                    @pl.when(there)
                    def _():
                        arrival(far, block, piece).wait()
                        relay_copy(block, target, piece).start()

        def arrival(slot, block, piece):
            part = held_ref.at[slot, block, rows(piece)]
            return pltpu.make_async_copy(part, part, recv_sem.at[slot, block, piece])

        def send_own(piece):
            for way, there in ((0, feat < n_feat - 1), (1, feat > 0)):

                @pl.when(there)
                def _():
                    copy(way, feat, piece, True).start()

            across(feat, piece, True, lambda each: each.start())

        def streams(step):
            return (
                (0, feat - step, feat >= step, feat < n_feat - 1),
                (1, feat + step, feat + step < n_feat, feat > 0),
            )

        def forward():
            for step in range(1, n_feat):
                for piece in range(pieces):
                    for way, block, there, onward in streams(step):

                        @pl.when(there)
                        def _():
                            arrival(1, block, piece).wait()

                            @pl.when(onward)
                            def _():
                                copy(way, block, piece, False).start()

                            across(block, piece, False, lambda each: each.start())

        def finish_sends():
            for piece in range(pieces):
                for way, there in ((0, feat < n_feat - 1), (1, feat > 0)):

                    @pl.when(there)
                    def _():
                        copy(way, feat, piece, True).wait_send()

                across(feat, piece, True, lambda each: each.wait_send())
                if piece < half:
                    for _, block, target, there in relays:

                        @pl.when(there)
                        def _():
                            relay_copy(block, target, piece).wait_send()

                for step in range(1, n_feat):
                    for way, block, there, onward in streams(step):

                        @pl.when(there)
                        def _():
                            @pl.when(onward)
                            def _():
                                copy(way, block, piece, False).wait_send()

                            across(block, piece, False, lambda each: each.wait_send())

        def arrive():
            for piece in range(pieces):
                for block in range(n_feat):
                    for slot in (0, 2):
                        passed_on = False
                        if piece < half:
                            for _, relay_block, _, there in relays:
                                if relay_block == block:
                                    passed_on = there & (far == slot)
                        pl.when(jnp.logical_not(passed_on))(
                            lambda slot=slot, block=block: arrival(slot, block, piece).wait()
                        )

        return send_own, forward, relay, finish_sends, arrive

    send_own, forward, relay, finish_one, arrive = gather(x_ref, panel, PIECES_ONE, send_one, recv_one)
    keep = pltpu.make_async_copy(x_ref, panel.at[1, feat], own_sem)
    for piece in range(PIECES_ONE):
        send_own(piece)
    keep.start()
    forward()
    relay()
    keep.wait()
    arrive()

    width = panel.shape[1] * panel.shape[2]
    hidden = layer_ref.shape[1]
    panel_tiles = panel.shape[3] // 128

    tiles_ref[3 * panel_tiles] = jnp.zeros((width, 128), tiles_ref.dtype)

    @pl.loop(0, panel_tiles)
    def _(at):
        column = pl.multiple_of(at * 128, 128)
        for slot in range(3):
            cells = panel[slot, :, :, pl.ds(column, 128)]
            tiles_ref[slot * panel_tiles + at] = cells.reshape(width, 128)

    def two_tiles(pair):
        def one_group(turn, carry):
            done = []
            for half in range(2):
                total, degree = carry[half]
                tile = pair * 2 + half
                first = turn * GROUP
                parts = [edge_ref[tile, first + lane] for lane in range(GROUP)]
                picked = [tiles_ref[where_ref[tile, first + lane]] for lane in range(GROUP)]
                total += lax.dot_general(
                    jnp.concatenate(parts, axis=1),
                    jnp.concatenate(picked, axis=1),
                    (((1,), (1,)), ((), ())),
                    preferred_element_type=jnp.float32,
                )
                for lane, part in enumerate(parts):
                    live = live_ref[pl.ds(tile * slots + first + lane, 1), :]
                    degree += part.astype(jnp.float32) * live
                done.append((total, degree))
            return tuple(done)

        zeros = (jnp.zeros((128, width), jnp.float32), jnp.zeros((128, 128), jnp.float32))
        sums = lax.fori_loop(0, slots // GROUP, one_group, (zeros, zeros))
        rest = jnp.concatenate([total for total, _ in sums], axis=0)
        degree = jnp.sum(
            jnp.concatenate([each for _, each in sums], axis=0), axis=1, keepdims=True
        )
        inv_root = lax.rsqrt(jnp.maximum(degree, 1.0))
        neighbour = jnp.zeros((256, hidden), jnp.float32)
        for _ in range(3):
            piece = rest.astype(jnp.bfloat16)
            rest = rest - piece.astype(jnp.float32)
            neighbour += jnp.dot(piece, wn_ref[...], preferred_element_type=jnp.float32)
        own = pl.multiple_of((feat * row_tiles + pair * 2) * 128, 256)
        self_one = lax.dot_general(
            panel[1, :, :, pl.ds(own, 256)].reshape(width, 256),
            ws_ref[...],
            (((0,), (0,)), ((), ())),
            preferred_element_type=jnp.float32,
        )
        layer = jnp.maximum(self_one + inv_root * neighbour + b_ref[...], 0.0)
        rows = pl.ds(pl.multiple_of(pair * 256, 256), 256)
        layer_ref[rows, :] = layer.astype(layer_ref.dtype)
        root_ref[rows, :] = jnp.broadcast_to(inv_root, (256, 128))

    send_own, forward, relay, finish_two, arrive = gather(
        layer_ref, out_ref, PIECES_TWO, send_two, recv_two
    )
    pairs = step_tiles // 2
    for piece in range(PIECES_TWO):
        edge_copy(piece).wait()
        pl.loop(piece * pairs, (piece + 1) * pairs)(two_tiles)
        send_own(piece)
    keep = pltpu.make_async_copy(layer_ref, out_ref.at[1, feat], own_sem)
    keep.start()
    forward()
    relay()
    keep.wait()
    finish_one()
    finish_two()
    arrive()


def second_kernel(
    where_ref, count_ref, first_ref, panel_ref, edge_ref, root_ref, cot_ref, ws_ref,
    wn_ref, b_ref, emb_ref, grad_ref, bias_ref,
):
    step = pl.program_id(0)
    hidden = emb_ref.shape[1]
    sums, own = [], []
    for half in range(2):
        tile = step * 2 + half
        count = count_ref[tile]

        def one_group(turn, total):
            first = turn * GROUP
            parts = live_group(edge_ref, half, first, count)
            picked = [panel_ref[where_ref[tile, first + lane]] for lane in range(GROUP)]
            return total + jnp.dot(
                jnp.concatenate(parts, axis=1),
                jnp.concatenate(picked, axis=0),
                preferred_element_type=jnp.float32,
            )

        zeros = jnp.zeros((128, hidden), jnp.float32)
        sums.append(lax.fori_loop(0, pl.cdiv(count, GROUP), one_group, zeros))
        own.append(panel_ref[first_ref[0] + tile])
    summed = jnp.concatenate(sums, axis=0)
    neighbour = (root_ref[:, :1] * summed).astype(jnp.bfloat16)
    layer = jnp.concatenate(own, axis=0)
    embedding = (
        jnp.dot(layer, ws_ref[...], preferred_element_type=jnp.float32)
        + jnp.dot(neighbour, wn_ref[...], preferred_element_type=jnp.float32)
        + b_ref[...]
    )
    emb_ref[...] = embedding.astype(emb_ref.dtype)
    cotangent = cot_ref[...]

    @pl.when(step == 0)
    def _():
        grad_ref[...] = jnp.zeros_like(grad_ref)
        bias_ref[...] = jnp.zeros_like(bias_ref)

    grad_ref[...] += lax.dot_general(
        jnp.concatenate([layer, neighbour], axis=1),
        cotangent,
        (((0,), (0,)), ((), ())),
        preferred_element_type=jnp.float32,
    )
    bias_ref[...] += jnp.sum(
        cotangent.astype(jnp.float32).reshape(-1, 8, cotangent.shape[1]), axis=0
    )


def reduce_kernel(
    n_dom, n_feat, g_ref, b_ref, out_ref, bias_ref,
    by_dom, bias_dom, by_feat, bias_feat, send_sem, recv_sem,
):
    dom, feat = lax.axis_index("dom"), lax.axis_index("feat")
    share = g_ref.shape[0] // n_dom

    def dom_at(step):
        return lax.rem(dom + step, n_dom)

    def feat_at(step):
        return lax.rem(feat + step, n_feat)

    def rows(index):
        return pl.ds(pl.multiple_of(index * share, share), share)

    def copy(kind, source, target, step, device_id):
        return pltpu.make_async_remote_copy(
            src_ref=source,
            dst_ref=target,
            send_sem=send_sem.at[kind, step],
            recv_sem=recv_sem.at[kind, step],
            device_id=device_id,
            device_id_type=MESH,
        )

    barrier = pltpu.get_barrier_semaphore()
    for step in range(1, n_dom):
        pl.semaphore_signal(
            barrier, inc=1, device_id=(dom_at(step), feat), device_id_type=MESH
        )
    for step in range(1, n_feat):
        pl.semaphore_signal(
            barrier, inc=1, device_id=(dom, feat_at(step)), device_id_type=MESH
        )
    pl.semaphore_wait(barrier, n_dom + n_feat - 2)

    scatter = []
    for step in range(1, n_dom):
        to = (dom_at(step), feat)
        scatter.append(copy(0, g_ref.at[rows(dom_at(step))], by_dom.at[dom], step, to))
        scatter.append(copy(1, b_ref, bias_dom.at[dom], step, to))
    for each in scatter:
        each.start()
    by_dom[dom] = g_ref[rows(dom), :]
    bias_dom[dom] = b_ref[...]
    for each in scatter:
        each.wait()
    by_feat[feat] = functools.reduce(lambda a, b: a + b, [by_dom[i] for i in range(n_dom)])
    bias_feat[feat] = functools.reduce(
        lambda a, b: a + b, [bias_dom[i] for i in range(n_dom)]
    )

    across = []
    for step in range(1, n_feat):
        to = (dom, feat_at(step))
        across.append(copy(2, by_feat.at[feat], by_feat.at[feat], step, to))
        across.append(copy(3, bias_feat.at[feat], bias_feat.at[feat], step, to))
    for each in across:
        each.start()
    for each in across:
        each.wait()
    out_ref[rows(dom), :] = functools.reduce(
        lambda a, b: a + b, [by_feat[i] for i in range(n_feat)]
    )
    bias_ref[...] = functools.reduce(lambda a, b: a + b, [bias_feat[i] for i in range(n_feat)])

    spread = [
        copy(4, out_ref.at[rows(dom)], out_ref.at[rows(dom)], step, (dom_at(step), feat))
        for step in range(1, n_dom)
    ]
    for each in spread:
        each.start()
    for each in spread:
        each.wait()


def reduce_all(grads, bias, n_dom, n_feat):
    share = grads.shape[0] // n_dom
    width = grads.shape[1]
    steps = max(n_dom, n_feat)
    whole = pl.BlockSpec(memory_space=pltpu.VMEM)
    return pl.pallas_call(
        functools.partial(reduce_kernel, n_dom, n_feat),
        out_shape=(
            jax.ShapeDtypeStruct(grads.shape, jnp.float32),
            jax.ShapeDtypeStruct(bias.shape, jnp.float32),
        ),
        in_specs=[whole] * 2,
        out_specs=(whole, whole),
        scratch_shapes=[
            pltpu.VMEM((n_dom, share, width), jnp.float32),
            pltpu.VMEM((n_dom,) + bias.shape, jnp.float32),
            pltpu.VMEM((n_feat, share, width), jnp.float32),
            pltpu.VMEM((n_feat,) + bias.shape, jnp.float32),
            pltpu.SemaphoreType.DMA((5, steps)),
            pltpu.SemaphoreType.DMA((5, steps)),
        ],
        compiler_params=pltpu.CompilerParams(
            collective_id=2, has_side_effects=True, vmem_limit_bytes=VMEM_LIMIT
        ),
        name="reduce_all",
    )(grads, bias)


def on_device(
    features, w1_self, w1_neigh, b1, w2_self, w2_neigh, b2, col_tiles, edge_weights, cotangent
):
    n_feat = lax.axis_size("feat")
    n_dom = lax.axis_size("dom")
    row_tiles, slots = col_tiles.shape
    panel_tiles = row_tiles * n_feat
    all_tiles = panel_tiles * n_dom
    hidden = w1_self.shape[1]
    occupied = col_tiles >= 0
    relative = jnp.mod(col_tiles - (lax.axis_index("dom") - 1) * panel_tiles, all_tiles)
    relative = jnp.where(occupied, relative, 3 * panel_tiles)
    live = jnp.broadcast_to(
        occupied.astype(jnp.float32).reshape(row_tiles * slots, 1), (row_tiles * slots, 128)
    )
    counts = jnp.sum(occupied.astype(jnp.int32), axis=1)
    first_own = jnp.full(
        (1,), panel_tiles + lax.axis_index("feat") * row_tiles, jnp.int32
    )
    rows = row_tiles * 128
    whole = pl.BlockSpec(memory_space=pltpu.VMEM)
    scalars = pl.BlockSpec(memory_space=pltpu.SMEM)
    anywhere = pl.BlockSpec(memory_space=pl.ANY)
    dma = pltpu.SemaphoreType.DMA

    panel_two, inv_root = pl.pallas_call(
        functools.partial(first_kernel, n_dom, n_feat),
        out_shape=(
            jax.ShapeDtypeStruct((3, n_feat, rows, hidden), jnp.bfloat16),
            jax.ShapeDtypeStruct((rows, 128), jnp.float32),
        ),
        in_specs=[anywhere, scalars, whole, anywhere, whole, whole, whole],
        out_specs=(anywhere, whole),
        scratch_shapes=[
            pltpu.VMEM((3, n_feat) + features.shape, jnp.bfloat16),
            pltpu.VMEM((3 * panel_tiles + 1, w1_self.shape[0], 128), jnp.bfloat16),
            pltpu.VMEM(edge_weights.shape, jnp.bfloat16),
            pltpu.VMEM((rows, hidden), jnp.bfloat16),
            dma,
            dma((PIECES_TWO,)),
            dma((5, n_feat, PIECES_ONE)),
            dma((3, n_feat, PIECES_ONE)),
            dma((5, n_feat, PIECES_TWO)),
            dma((3, n_feat, PIECES_TWO)),
        ],
        compiler_params=pltpu.CompilerParams(
            collective_id=0, has_side_effects=True, vmem_limit_bytes=VMEM_LIMIT
        ),
        name="first_layer",
    )(
        features,
        relative,
        live,
        edge_weights,
        w1_self,
        w1_neigh,
        b1[None],
    )

    def fixed(*shape):
        return pl.BlockSpec(
            shape, lambda r, *_: (0,) * len(shape), pipeline_mode=pl.Buffered(1)
        )

    def by_step(width):
        return pl.BlockSpec((256, width), lambda r, *_: (r, 0))

    panel_two = panel_two.reshape(3 * panel_tiles, 128, hidden)
    embedding, grads, bias = pl.pallas_call(
        second_kernel,
        grid_spec=pltpu.PrefetchScalarGridSpec(
            num_scalar_prefetch=3,
            grid=(row_tiles // 2,),
            in_specs=[
                fixed(3 * panel_tiles, 128, hidden),
                pl.BlockSpec((2, slots, 128, 128), lambda r, *_: (r, 0, 0, 0)),
                by_step(128),
                by_step(hidden),
                fixed(hidden, hidden),
                fixed(hidden, hidden),
                fixed(1, hidden),
            ],
            out_specs=(
                by_step(hidden),
                pl.BlockSpec((2 * hidden, hidden), lambda r, *_: (0, 0)),
                pl.BlockSpec((8, hidden), lambda r, *_: (0, 0)),
            ),
        ),
        out_shape=(
            jax.ShapeDtypeStruct((rows, hidden), jnp.bfloat16),
            jax.ShapeDtypeStruct((2 * hidden, hidden), jnp.float32),
            jax.ShapeDtypeStruct((8, hidden), jnp.float32),
        ),
        compiler_params=pltpu.CompilerParams(vmem_limit_bytes=VMEM_LIMIT),
        name="second_layer",
    )(
        jnp.where(occupied, relative, 0), counts, first_own, panel_two, edge_weights, inv_root, cotangent,
        w2_self, w2_neigh, b2[None],
    )
    grads, bias = reduce_all(grads, bias, n_dom, n_feat)
    return (embedding, grads[:hidden], grads[hidden:], jnp.sum(bias, axis=0))


def solution(mesh):
    placed = (
        P("feat", "dom"),
        P(),
        P(),
        P(),
        P(),
        P(),
        P(),
        P(("dom", "feat"), None),
        P(("dom", "feat"), None, None, None),
        P(("dom", "feat"), None),
    )
    return jax.shard_map(
        on_device,
        mesh=mesh,
        in_specs=placed,
        out_specs=(P(("dom", "feat"), None), P(), P(), P()),
        check_vma=False,
    )
```
